32 devices in a mesh: user: 4 (over x, core), item: 8 (over z, y).
Axes of the slice: x: 2, y: 2, z: 4, core: 2. Of those that a mesh axis runs over, the one named last changes fastest.
Arguments:
- user_factors: float32 [8192, 256], P(('user', 'item')), may hold values from -6 to 6
- item_factors: bfloat16 [32768, 256], P('item')
- head_ids: int32 [8], replicated, may hold values from 0 to 127, as said below
- tail_ids: int32 [32, 16], P(('user', 'item')), may hold values from 0 to 127, as said below
- head_counts: int32 [32, 8, 256, 256], P(('user', 'item')), may hold values from 0 to 7
- tail_counts: int32 [32, 16, 256, 256], P(('user', 'item')), may hold values from 0 to 7
Outputs:
- new_factors: float32 [8192, 256], P(('user', 'item'))
- residual: float32 [8192, 256], P(('user', 'item'))
The draws below stay inside these ranges and needn't reach their ends.
Inputs may be any that keep to these rules, and one draw needn't show every extreme that they name: `head_ids`: 8 distinct block numbers, among them 0 and 127. `tail_ids`: each row holds distinct block numbers; at most 4 of a row fall in the range of one index of item (blocks o * 16 to (o + 1) * 16 - 1), and one range, the same for every row, holds exactly 4 of every row.
All inputs are finite; a program needn't handle non-finite values.
Results may differ from the reference program's by a relative error of at most 0.0055.
Values may be sent and summed in bfloat16 or wider, within the bound.
A program may use at most 128 MiB of HBM per device.

```python
import math
import jax
import jax.numpy as jnp
from jax import lax

F = 256
BLK = 256
ITERS = 2
HEAD_B = 8
TAIL_K = 16
NUM_ITEMS = 32768
SHARD_BLOCKS = 16
ITEM_BLOCKS = 128
CAP = 4
USER_BLOCKS = 32
USERS = 8192


def draw_item_factors(key, part):
    key_col, key_row, key_noise = jax.random.split(key, 3)
    column_scale = jnp.exp(jax.random.uniform(key_col, (1, F), minval=math.log(0.3), maxval=math.log(3.0)))
    row_scale = jnp.exp(jax.random.uniform(key_row, (NUM_ITEMS, 1), minval=0.0, maxval=math.log(3.0)))
    position = jnp.arange(NUM_ITEMS, dtype=jnp.float32).reshape(NUM_ITEMS, 1)
    row_scale = row_scale * (1.0 + 2.0 * position / NUM_ITEMS)
    noise = jax.random.normal(key_noise, (NUM_ITEMS, F))
    values = noise * column_scale * row_scale / math.sqrt(NUM_ITEMS)
    return values.astype(jnp.float32).astype(jnp.bfloat16)


def draw_head_ids(key, part):
    key_pick, key_order = jax.random.split(jax.random.fold_in(key, 3))
    middle = jax.random.permutation(key_pick, ITEM_BLOCKS - 2)[:HEAD_B - 2] + 1
    ends = jnp.array([0, ITEM_BLOCKS - 1], dtype=jnp.int32)
    chosen = jnp.concatenate([ends, middle.astype(jnp.int32)])
    return chosen[jax.random.permutation(key_order, HEAD_B)].astype(jnp.int32)


def draw_tail_ids(key, part):
    hot_key, rest_key = jax.random.split(jax.random.fold_in(key, 7))
    owner_total = ITEM_BLOCKS // SHARD_BLOCKS
    slot_total = owner_total * CAP
    hot_owner = jax.random.randint(hot_key, (), 0, owner_total)

    def draw_row(row_key):
        key_order, key_band, key_shuffle = jax.random.split(row_key, 3)
        order_rank = jax.random.permutation(key_order, slot_total)
        slot_owner = jnp.arange(slot_total) // CAP
        score_int = jnp.where(slot_owner == hot_owner, 0, 1) * slot_total + order_rank
        chosen = jnp.argsort(score_int)[:TAIL_K]
        pick_owner = chosen // CAP
        within = chosen % CAP
        band_index = jax.random.randint(key_band, (TAIL_K,), 0, SHARD_BLOCKS // CAP)
        block_ids = pick_owner * SHARD_BLOCKS + band_index * CAP + within
        return block_ids[jax.random.permutation(key_shuffle, TAIL_K)]
    row_keys = jax.random.split(rest_key, USER_BLOCKS)
    return jax.vmap(draw_row)(row_keys).astype(jnp.int32)


def plant(values, rng, least, top_value):
    index_at = [jax.random.randint(jax.random.fold_in(rng, axis), (), 0, length) for axis, length in enumerate(values.shape)]
    widest = values.shape.index(max(values.shape))
    neighbour = index_at[:widest] + [(index_at[widest] + 1) % values.shape[widest]] + index_at[widest + 1:]
    return values.at[tuple(index_at)].set(least).at[tuple(neighbour)].set(top_value)


def block_levels(rng, shape, shards, smallest, largest):
    level = 1.0
    for dim, parts in shards:
        steps = jax.random.uniform(jax.random.fold_in(jax.random.fold_in(rng, 6), dim), (parts,), jnp.float32, smallest / len(shards), largest / len(shards))
        level = level * jnp.repeat(jnp.exp(steps), shape[dim] // parts).reshape((-1,) + (1,) * (len(shape) - 1 - dim))
    return level


def scatter_about(key, extent, spread, limit, cuts=(), kind=jnp.bfloat16):
    entries = jax.random.normal(key, extent, jnp.float32) * spread
    if len(cuts) > 0:
        entries = block_levels(key, extent, cuts, -0.22, 0.18) * entries
    return jnp.clip(entries, min=-limit, max=limit).astype(kind)


def setup_inputs(seed: int = 0) -> dict:
    key_of = jax.random.split(jax.random.key(seed), 7)
    user_factors = scatter_about(key_of[0], (USERS, F), 1.0, 6.0, ((0, 32),), jnp.float32)
    item_factors = draw_item_factors(jax.random.fold_in(key_of[6], 71), 0)
    head_ids = draw_head_ids(jax.random.fold_in(key_of[6], 71), 0)
    tail_ids = draw_tail_ids(jax.random.fold_in(key_of[6], 71), 0)
    head_counts = plant(jax.random.randint(key_of[4], (USER_BLOCKS, HEAD_B, BLK, BLK), 0, 8), jax.random.fold_in(key_of[4], 1), 0, 7).astype(jnp.int32)
    tail_counts = plant(jax.random.randint(key_of[5], (USER_BLOCKS, TAIL_K, BLK, BLK), 0, 8), jax.random.fold_in(key_of[5], 1), 0, 7).astype(jnp.int32)
    return {"user_factors": user_factors, "item_factors": item_factors, "head_ids": head_ids, "tail_ids": tail_ids, "head_counts": head_counts, "tail_counts": tail_counts}


conf_alpha = 4.0
ridge_term = 0.1
epsilon = 1e-6


def apply_operator(vector, gram_matrix, item_tiles, weights):
    rounded = vector.astype(jnp.bfloat16)
    scores = jnp.einsum('uf,kif->kui', rounded.astype(jnp.float32), item_tiles.astype(jnp.float32))
    scaled = (scores * weights.astype(jnp.float32)).astype(jnp.bfloat16)
    data_term = jnp.einsum('kui,kif->uf', scaled.astype(jnp.float32), item_tiles.astype(jnp.float32))
    gram_term = jnp.dot(vector, gram_matrix, precision=lax.Precision.HIGHEST)
    return gram_term + ridge_term * vector + data_term


def solve_block(start_vec, gram_matrix, item_tiles, counts):
    count_float = counts.astype(jnp.float32)
    weights = (conf_alpha * count_float).astype(jnp.bfloat16)
    rated_weight = jnp.where(counts > 0, 1.0 + conf_alpha * count_float, 0.0).astype(jnp.bfloat16)
    rhs = jnp.einsum('kui,kif->uf', rated_weight.astype(jnp.float32), item_tiles.astype(jnp.float32))
    solution = start_vec
    residual = rhs - apply_operator(solution, gram_matrix, item_tiles, weights)
    direction = residual
    norm_now = jnp.sum(residual * residual, axis=1, keepdims=True)
    for turn_index in range(ITERS):
        image_vec = apply_operator(direction, gram_matrix, item_tiles, weights)
        step_size = norm_now / (jnp.sum(direction * image_vec, axis=1, keepdims=True) + epsilon)
        solution = solution + step_size * direction
        residual = residual - step_size * image_vec
        if turn_index + 1 < ITERS:
            norm_next = jnp.sum(residual * residual, axis=1, keepdims=True)
            direction = residual + (norm_next / (norm_now + epsilon)) * direction
            norm_now = norm_next
    return solution, residual


def reference(user_factors, item_factors, head_ids, tail_ids, head_counts, tail_counts):
    gram_matrix = jnp.dot(item_factors.T, item_factors, preferred_element_type=jnp.float32)
    blocks = item_factors.reshape(ITEM_BLOCKS, BLK, F)
    head_rows = blocks[head_ids]

    def one_block(block_args):
        start_vec, tail_list, head_part, tail_part = block_args
        item_tiles = jnp.concatenate([head_rows, blocks[tail_list]], axis=0)
        counts = jnp.concatenate([head_part, tail_part], axis=0)
        return solve_block(start_vec, gram_matrix, item_tiles, counts)

    user_blocks = user_factors.reshape(USER_BLOCKS, BLK, F)
    solution, residual = lax.map(one_block, (user_blocks, tail_ids, head_counts, tail_counts))
    return solution.reshape(USERS, F), residual.reshape(USERS, F)
```

```python
import jax
import jax.numpy as jnp
from jax import lax
from jax.experimental import pallas as pl
from jax.experimental.pallas import tpu as pltpu
from jax.sharding import PartitionSpec as P

ITERS = 2


conf_alpha = 4.0
ridge_term = 0.1
epsilon = 1e-06


def apply_operator(vector, gram_matrix, item_tiles, weights):
    rounded = vector.astype(jnp.bfloat16)
    scores = jnp.einsum("uf,kif->kui", rounded, item_tiles, preferred_element_type=jnp.float32)
    scaled = (scores * weights).astype(jnp.bfloat16)
    data_term = jnp.einsum("kui,kif->uf", scaled, item_tiles, preferred_element_type=jnp.float32)
    gram_term = jnp.dot(vector, gram_matrix, precision=lax.Precision.HIGHEST)
    return gram_term + ridge_term * vector + data_term


def solve_block(start_vec, gram_matrix, item_tiles, counts):
    count_float = counts.astype(jnp.float32)
    weights = (conf_alpha * count_float).astype(jnp.bfloat16)
    rated_weight = jnp.where(counts > 0, 1.0 + conf_alpha * count_float, 0.0).astype(jnp.bfloat16)
    rhs = jnp.einsum("kui,kif->uf", rated_weight, item_tiles, preferred_element_type=jnp.float32)
    solution = start_vec
    residual = rhs - apply_operator(solution, gram_matrix, item_tiles, weights)
    direction = residual
    norm_now = jnp.sum(residual * residual, axis=1, keepdims=True)
    for turn_index in range(ITERS):
        image_vec = apply_operator(direction, gram_matrix, item_tiles, weights)
        step_size = norm_now / (jnp.sum(direction * image_vec, axis=1, keepdims=True) + epsilon)
        solution = solution + step_size * direction
        residual = residual - step_size * image_vec
        if turn_index + 1 < ITERS:
            norm_next = jnp.sum(residual * residual, axis=1, keepdims=True)
            direction = residual + norm_next / (norm_now + epsilon) * direction
            norm_now = norm_next
    return (solution, residual)


def take_blocks(blocks, ids):
    return jnp.stack(
        [lax.dynamic_index_in_dim(blocks, ids[k], 0, keepdims=False) for k in range(ids.shape[0])]
    )


def local(user_factors, item_factors, head_ids, tail_ids, head_counts, tail_counts):
    item_count = lax.axis_size("item")
    user_count = lax.axis_size("user")
    block_size = head_counts.shape[-1]
    rank_width = item_factors.shape[1]
    shard_blocks = item_factors.shape[0] // block_size
    blocks = item_factors.reshape(shard_blocks, block_size, rank_width)
    my_item = lax.axis_index("item")
    contract = (((0,), (0,)), ((), ()))
    slice_rows = item_factors.shape[0] // user_count
    rows_part = lax.dynamic_slice_in_dim(
        item_factors, lax.axis_index("user") * slice_rows, slice_rows, 0
    )
    local_gram = lax.dot_general(rows_part, rows_part, contract, preferred_element_type=jnp.float32)
    gram_matrix = lax.psum(local_gram, ("user", "item"))
    head_owner = head_ids // shard_blocks
    head_local = head_ids % shard_blocks
    owned = head_owner == my_item
    picked = jnp.where(owned[:, None, None], take_blocks(blocks, head_local), jnp.zeros((), jnp.bfloat16))
    head_rows = lax.psum(picked, "item").astype(jnp.float32).astype(jnp.bfloat16)
    wanted = tail_ids.reshape(-1)
    length = wanted.shape[0]
    capacity = 2 * length // item_count
    owner_of = wanted // shard_blocks
    local_of = wanted % shard_blocks
    same_owner = owner_of[:, None] == owner_of[None, :]
    positions = jnp.arange(length, dtype=jnp.int32)
    earlier = positions[:, None] > positions[None, :]
    place_index = jnp.sum((same_owner & earlier).astype(jnp.int32), axis=1)
    slot_index = owner_of * capacity + place_index
    slot_table = slot_index[:, None] == jnp.arange(item_count * capacity, dtype=jnp.int32)[None, :]
    requests = jnp.sum(jnp.where(slot_table, local_of[:, None], 0), axis=0)
    requests = requests.reshape(item_count, capacity)
    asked = lax.all_to_all(requests, "item", split_axis=0, concat_axis=0, tiled=True)
    served = take_blocks(blocks, asked.reshape(-1)).reshape(item_count, capacity, block_size, rank_width)
    arrived_tail = lax.all_to_all(served, "item", split_axis=0, concat_axis=0, tiled=True)
    tail_rows = take_blocks(
        arrived_tail.reshape(item_count * capacity, block_size, rank_width), slot_index
    )
    local_blocks = tail_ids.shape[0]
    tail_tiles = tail_rows.reshape(local_blocks, tail_ids.shape[1], block_size, rank_width)
    start_blocks = user_factors.reshape(local_blocks, block_size, rank_width)

    def one_block(block_args):
        start_vec, tail_part_rows, head_part, tail_part = block_args
        item_tiles = jnp.concatenate([head_rows, tail_part_rows], axis=0)
        counts = jnp.concatenate([head_part, tail_part], axis=0)
        return solve_block(start_vec, gram_matrix, item_tiles, counts)

    solution, residual = lax.map(one_block, (start_blocks, tail_tiles, head_counts, tail_counts))
    return (
        solution.reshape(local_blocks * block_size, rank_width),
        residual.reshape(local_blocks * block_size, rank_width),
    )


PARTS = 2
STEPS = (1, 3, 2)


def gather_kernel(shard, out, send_sem, recv_sem, own_sem):
    user, item = lax.axis_index("user"), lax.axis_index("item")
    x, c = user // 2, user % 2
    z, y = item // 2, item % 2
    rows = shard.shape[1] // PARTS

    def dev(x_at, y_at, z_at, c_at):
        return (x_at * 2 + c_at, z_at * 2 + y_at)

    side_x, side_y, side_c = dev(1 - x, y, z, c), dev(x, 1 - y, z, c), dev(x, y, z, 1 - c)
    barrier = pltpu.get_barrier_semaphore()
    for other in [side_x, side_y, side_c] + [dev(x, y, (z + r) % 4, c) for r in STEPS]:
        pl.semaphore_signal(barrier, inc=1, device_id=other, device_id_type=pl.DeviceIdType.MESH)
    pl.semaphore_wait(barrier, 6)

    def place(z_at, y_at, x_at, part):
        return out.at[z_at * 2 + y_at, x_at * 2 + c, pl.ds(part * rows, rows)]

    slots = {}

    def slot(name):
        return slots.setdefault(name, len(slots))

    def copy(name, source, target, device):
        return pltpu.make_async_remote_copy(
            src_ref=source,
            dst_ref=target,
            send_sem=send_sem.at[slot(name)],
            recv_sem=recv_sem.at[slot(name)],
            device_id=device,
            device_id_type=pl.DeviceIdType.MESH,
        )

    started = []

    def send(name, source, target, device):
        made = copy(name, source, target, device)
        made.start()
        started.append(made)

    def arrive(name, target):
        copy(name, target, target, side_c).wait_recv()

    def pass_on(name, target):
        send(("c",) + name, target, target, side_c)

    own = pltpu.make_async_copy(shard, out.at[item], own_sem)
    own.start()
    for part in range(PARTS):
        piece = shard.at[x * 2 + c, pl.ds(part * rows, rows)]
        far = shard.at[(1 - x) * 2 + c, pl.ds(part * rows, rows)]
        for r in STEPS:
            send(("z", r, part), piece, place(z, y, x, part), dev(x, y, (z + r) % 4, c))
        send(("y", 0, part), piece, place(z, y, x, part), side_y)
        send(("d", 0, part), far, place(z, y, 1 - x, part), side_y)
    landed = []

    def take(name, target):
        arrive(name, target)
        pass_on(name, target)
        landed.append((("c",) + name, name))

    for part in range(PARTS):
        for r in STEPS:
            here = place((z + 4 - r) % 4, y, x, part)
            arrive(("z", r, part), here)
            send(("x", r, part), here, here, side_x)
            send(("y", r, part), here, here, side_y)
            pass_on(("z", r, part), here)
        take(("y", 0, part), place(z, 1 - y, x, part))
        take(("d", 0, part), place(z, 1 - y, 1 - x, part))
    for part in range(PARTS):
        for r in STEPS:
            plane = (z + 4 - r) % 4
            from_x = place(plane, y, 1 - x, part)
            from_y = place(plane, 1 - y, x, part)
            by_x = r == 1 or (r == 2 and part % 2 == 0) or (r == 3 and part % 2 == 0)
            arrive(("x", r, part), from_x)
            if not by_x:
                send(("d", r, part), from_x, from_x, side_y)
            pass_on(("x", r, part), from_x)
            arrive(("y", r, part), from_y)
            if by_x:
                send(("d", r, part), from_y, from_y, side_x)
            pass_on(("y", r, part), from_y)
    for part in range(PARTS):
        for r in STEPS:
            take(("d", r, part), place((z + 4 - r) % 4, 1 - y, 1 - x, part))

    def other_core(z_at, y_at, x_at, part):
        return out.at[z_at * 2 + y_at, x_at * 2 + 1 - c, pl.ds(part * rows, rows)]

    for part in range(PARTS):
        arrive(("c", "y", 0, part), other_core(z, 1 - y, x, part))
        arrive(("c", "d", 0, part), other_core(z, 1 - y, 1 - x, part))
        for r in STEPS:
            plane = (z + 4 - r) % 4
            arrive(("c", "z", r, part), other_core(plane, y, x, part))
            arrive(("c", "x", r, part), other_core(plane, y, 1 - x, part))
            arrive(("c", "y", r, part), other_core(plane, 1 - y, x, part))
            arrive(("c", "d", r, part), other_core(plane, 1 - y, 1 - x, part))
    for made in started:
        made.wait_send()
    own.wait()


COPIES = PARTS * (3 + 3 + 4 + 4 + 14)


def gather_all(item_factors, item_count):
    rows, width = item_factors.shape
    shard = item_factors.reshape(4, rows // 4, width)
    return pl.pallas_call(
        gather_kernel,
        out_shape=jax.ShapeDtypeStruct((item_count, 4, rows // 4, width), item_factors.dtype),
        in_specs=[pl.BlockSpec(memory_space=pl.ANY)],
        out_specs=pl.BlockSpec(memory_space=pl.ANY),
        scratch_shapes=[
            pltpu.SemaphoreType.DMA((COPIES,)),
            pltpu.SemaphoreType.DMA((COPIES,)),
            pltpu.SemaphoreType.DMA,
        ],
        compiler_params=pltpu.CompilerParams(collective_id=0, has_side_effects=True),
    )(shard)


GROUP = 4


def solve_kernel(
    head_ids, tail_ids, start, gram, head_counts, tail_counts, items, out, residual_out, tiles, weights, acc, sem
):
    head_count, tail_count = head_counts.shape[0], tail_counts.shape[0]
    total = head_count + tail_count
    size, width = tiles.shape[1], tiles.shape[2]

    def fetch(k):
        block = head_ids[k] if k < head_count else tail_ids[k - head_count]
        return pltpu.make_async_copy(items.at[block], tiles.at[k], sem.at[k])

    for k in range(total):
        fetch(k).start()
    last = (((1,), (1,)), ((), ()))

    def group_tiles(g):
        return tiles[pl.ds(g * GROUP, GROUP)].reshape(GROUP * size, width)

    def data_part(rounded, rows, weight):
        scores = lax.dot_general(rounded, rows, last, preferred_element_type=jnp.float32)
        scaled = (scores * weight.astype(jnp.float32)).astype(jnp.bfloat16)
        return jnp.dot(scaled, rows, preferred_element_type=jnp.float32)

    def dense_part(vector):
        image = jnp.dot(
            vector, gram[...], precision=lax.Precision.HIGHEST, preferred_element_type=jnp.float32
        )
        return image + ridge_term * vector

    start_vec = start[...]
    acc[...] = -dense_part(start_vec)
    rounded_start = start_vec.astype(jnp.bfloat16)
    for k in range(total):
        fetch(k).wait()

    def first(counts, base):
        def body(g, carry):
            weight_list, rated_list = [], []
            for k in range(GROUP):
                count = counts[g * GROUP + k].astype(jnp.float32)
                weight = conf_alpha * count
                weight_list.append(weight.astype(jnp.bfloat16))
                rated_list.append(jnp.where(count > 0, 1.0 + weight, 0.0).astype(jnp.bfloat16))
            weight = jnp.concatenate(weight_list, axis=1)
            rated = jnp.concatenate(rated_list, axis=1)
            weights[base + g] = weight
            rows = group_tiles(base + g)
            acc[...] += jnp.dot(rated, rows, preferred_element_type=jnp.float32) - data_part(
                rounded_start, rows, weight
            )
            return carry

        lax.fori_loop(0, counts.shape[0] // GROUP, body, 0)

    first(head_counts, 0)
    first(tail_counts, head_count // GROUP)

    def apply(vector):
        acc[...] = dense_part(vector)
        rounded = vector.astype(jnp.bfloat16)

        def body(g, carry):
            acc[...] += data_part(rounded, group_tiles(g), weights[g])
            return carry

        lax.fori_loop(0, total // GROUP, body, 0)
        return acc[...]

    solution = start_vec
    residual = acc[...]
    direction = residual
    norm_now = jnp.sum(residual * residual, axis=1, keepdims=True)
    for turn_index in range(ITERS):
        image_vec = apply(direction)
        step_size = norm_now / (jnp.sum(direction * image_vec, axis=1, keepdims=True) + epsilon)
        solution = solution + step_size * direction
        residual = residual - step_size * image_vec
        if turn_index + 1 < ITERS:
            norm_next = jnp.sum(residual * residual, axis=1, keepdims=True)
            direction = residual + norm_next / (norm_now + epsilon) * direction
            norm_now = norm_next
    out[...] = solution
    residual_out[...] = residual


def local_gathered(user_factors, item_factors, head_ids, tail_ids, head_counts, tail_counts):
    size, width = head_counts.shape[-1], item_factors.shape[1]
    items = gather_all(item_factors, lax.axis_size("item"))
    flat = items.reshape(-1, width)
    gram_matrix = lax.dot_general(
        flat, flat, (((0,), (0,)), ((), ())), preferred_element_type=jnp.float32
    )
    total = head_counts.shape[1] + tail_counts.shape[1]
    smem = pl.BlockSpec(memory_space=pltpu.SMEM)
    vmem = pl.BlockSpec(memory_space=pltpu.VMEM)
    shape = jax.ShapeDtypeStruct(user_factors.shape, jnp.float32)
    return pl.pallas_call(
        solve_kernel,
        out_shape=(shape, shape),
        in_specs=[smem, smem, vmem, vmem, vmem, vmem, pl.BlockSpec(memory_space=pl.ANY)],
        out_specs=(vmem, vmem),
        scratch_shapes=[
            pltpu.VMEM((total, size, width), jnp.bfloat16),
            pltpu.VMEM((total // GROUP, size, GROUP * size), jnp.bfloat16),
            pltpu.VMEM((size, width), jnp.float32),
            pltpu.SemaphoreType.DMA((total,)),
        ],
        compiler_params=pltpu.CompilerParams(vmem_limit_bytes=40 * 1024 * 1024),
    )(
        head_ids,
        tail_ids.reshape(-1),
        user_factors,
        gram_matrix,
        head_counts[0],
        tail_counts[0],
        items.reshape(-1, size, width),
    )


def solution(mesh):
    small = mesh.shape["user"] == 4 and mesh.shape["item"] == 8
    return jax.shard_map(
        local_gathered if small else local,
        mesh=mesh,
        in_specs=(
            P(("user", "item"), None),
            P("item", None),
            P(),
            P(("user", "item"), None),
            P(("user", "item"), None, None, None),
            P(("user", "item"), None, None, None),
        ),
        out_specs=(P(("user", "item"), None), P(("user", "item"), None)),
        check_vma=False,
    )
```

```python
import jax
import jax.numpy as jnp
from jax import lax
from jax.experimental import pallas as pl
from jax.experimental.pallas import tpu as pltpu
from jax.sharding import PartitionSpec as P

ITERS = 2


conf_alpha = 4.0
ridge_term = 0.1
epsilon = 1e-06


def apply_operator(vector, gram_matrix, item_tiles, weights):
    rounded = vector.astype(jnp.bfloat16)
    scores = jnp.einsum("uf,kif->kui", rounded, item_tiles, preferred_element_type=jnp.float32)
    scaled = (scores * weights).astype(jnp.bfloat16)
    data_term = jnp.einsum("kui,kif->uf", scaled, item_tiles, preferred_element_type=jnp.float32)
    gram_term = jnp.dot(vector, gram_matrix, precision=lax.Precision.HIGHEST)
    return gram_term + ridge_term * vector + data_term


def solve_block(start_vec, gram_matrix, item_tiles, counts):
    count_float = counts.astype(jnp.float32)
    weights = (conf_alpha * count_float).astype(jnp.bfloat16)
    rated_weight = jnp.where(counts > 0, 1.0 + conf_alpha * count_float, 0.0).astype(jnp.bfloat16)
    rhs = jnp.einsum("kui,kif->uf", rated_weight, item_tiles, preferred_element_type=jnp.float32)
    solution = start_vec
    residual = rhs - apply_operator(solution, gram_matrix, item_tiles, weights)
    direction = residual
    norm_now = jnp.sum(residual * residual, axis=1, keepdims=True)
    for turn_index in range(ITERS):
        image_vec = apply_operator(direction, gram_matrix, item_tiles, weights)
        step_size = norm_now / (jnp.sum(direction * image_vec, axis=1, keepdims=True) + epsilon)
        solution = solution + step_size * direction
        residual = residual - step_size * image_vec
        if turn_index + 1 < ITERS:
            norm_next = jnp.sum(residual * residual, axis=1, keepdims=True)
            direction = residual + norm_next / (norm_now + epsilon) * direction
            norm_now = norm_next
    return (solution, residual)


def take_blocks(blocks, ids):
    return jnp.stack(
        [lax.dynamic_index_in_dim(blocks, ids[k], 0, keepdims=False) for k in range(ids.shape[0])]
    )


def local(user_factors, item_factors, head_ids, tail_ids, head_counts, tail_counts):
    item_count = lax.axis_size("item")
    user_count = lax.axis_size("user")
    block_size = head_counts.shape[-1]
    rank_width = item_factors.shape[1]
    shard_blocks = item_factors.shape[0] // block_size
    blocks = item_factors.reshape(shard_blocks, block_size, rank_width)
    my_item = lax.axis_index("item")
    contract = (((0,), (0,)), ((), ()))
    slice_rows = item_factors.shape[0] // user_count
    rows_part = lax.dynamic_slice_in_dim(
        item_factors, lax.axis_index("user") * slice_rows, slice_rows, 0
    )
    local_gram = lax.dot_general(rows_part, rows_part, contract, preferred_element_type=jnp.float32)
    gram_matrix = lax.psum(local_gram, ("user", "item"))
    head_owner = head_ids // shard_blocks
    head_local = head_ids % shard_blocks
    owned = head_owner == my_item
    picked = jnp.where(owned[:, None, None], take_blocks(blocks, head_local), jnp.zeros((), jnp.bfloat16))
    head_rows = lax.psum(picked, "item").astype(jnp.float32).astype(jnp.bfloat16)
    wanted = tail_ids.reshape(-1)
    length = wanted.shape[0]
    capacity = 2 * length // item_count
    owner_of = wanted // shard_blocks
    local_of = wanted % shard_blocks
    same_owner = owner_of[:, None] == owner_of[None, :]
    positions = jnp.arange(length, dtype=jnp.int32)
    earlier = positions[:, None] > positions[None, :]
    place_index = jnp.sum((same_owner & earlier).astype(jnp.int32), axis=1)
    slot_index = owner_of * capacity + place_index
    slot_table = slot_index[:, None] == jnp.arange(item_count * capacity, dtype=jnp.int32)[None, :]
    requests = jnp.sum(jnp.where(slot_table, local_of[:, None], 0), axis=0)
    requests = requests.reshape(item_count, capacity)
    asked = lax.all_to_all(requests, "item", split_axis=0, concat_axis=0, tiled=True)
    served = take_blocks(blocks, asked.reshape(-1)).reshape(item_count, capacity, block_size, rank_width)
    arrived_tail = lax.all_to_all(served, "item", split_axis=0, concat_axis=0, tiled=True)
    tail_rows = take_blocks(
        arrived_tail.reshape(item_count * capacity, block_size, rank_width), slot_index
    )
    local_blocks = tail_ids.shape[0]
    tail_tiles = tail_rows.reshape(local_blocks, tail_ids.shape[1], block_size, rank_width)
    start_blocks = user_factors.reshape(local_blocks, block_size, rank_width)

    def one_block(block_args):
        start_vec, tail_part_rows, head_part, tail_part = block_args
        item_tiles = jnp.concatenate([head_rows, tail_part_rows], axis=0)
        counts = jnp.concatenate([head_part, tail_part], axis=0)
        return solve_block(start_vec, gram_matrix, item_tiles, counts)

    solution, residual = lax.map(one_block, (start_blocks, tail_tiles, head_counts, tail_counts))
    return (
        solution.reshape(local_blocks * block_size, rank_width),
        residual.reshape(local_blocks * block_size, rank_width),
    )


PARTS = 4
STEPS = (1, 3, 2)
GROUP = 4
COPIES = PARTS * (3 + 3 + 4 + 4 + 14) + 1


def solve_kernel(
    head_ids, tail_ids, start, shard, head_counts, tail_counts, out, residual_out,
    items, head_held, tail_held, weights, rated, gram, gram_other, acc,
    send_sem, recv_sem, own_sem,
):
    user, item = lax.axis_index("user"), lax.axis_index("item")
    x, c = user // 2, user % 2
    z, y = item // 2, item % 2
    shard_blocks, size, width = shard.shape
    quarter = shard_blocks // 4
    run = quarter // PARTS
    heads, tails = head_counts.shape[0], tail_counts.shape[0]

    def dev(x_at, y_at, z_at, c_at):
        return (x_at * 2 + c_at, z_at * 2 + y_at)

    side_x, side_y, side_c = dev(1 - x, y, z, c), dev(x, 1 - y, z, c), dev(x, y, z, 1 - c)
    barrier = pltpu.get_barrier_semaphore()
    for other in [side_x, side_y, side_c] + [dev(x, y, (z + r) % 4, c) for r in STEPS]:
        pl.semaphore_signal(barrier, inc=1, device_id=other, device_id_type=pl.DeviceIdType.MESH)
    own = pltpu.make_async_copy(shard, items.at[pl.ds(item * shard_blocks, shard_blocks)], own_sem.at[0])
    head_in = pltpu.make_async_copy(head_counts, head_held, own_sem.at[1])
    tail_in = pltpu.make_async_copy(tail_counts, tail_held, own_sem.at[2])
    own.start()
    pl.semaphore_wait(barrier, 6)

    def first_block(z_at, y_at, x_at, part, core):
        return (z_at * 2 + y_at) * shard_blocks + (x_at * 2 + core) * quarter + part * run

    def place(z_at, y_at, x_at, part):
        return items.at[pl.ds(first_block(z_at, y_at, x_at, part, c), run)]

    def other_core(z_at, y_at, x_at, part):
        return items.at[pl.ds(first_block(z_at, y_at, x_at, part, 1 - c), run)]

    slots = {}

    def slot(name):
        return slots.setdefault(name, len(slots))

    def copy(name, source, target, device):
        return pltpu.make_async_remote_copy(
            src_ref=source,
            dst_ref=target,
            send_sem=send_sem.at[slot(name)],
            recv_sem=recv_sem.at[slot(name)],
            device_id=device,
            device_id_type=pl.DeviceIdType.MESH,
        )

    started = []

    def send(name, source, target, device):
        made = copy(name, source, target, device)
        made.start()
        started.append(made)

    def arrive(name, target):
        copy(name, target, target, side_c).wait_recv()

    def pass_on(name, target):
        send(("c",) + name, target, target, side_c)

    def take(name, target):
        arrive(name, target)
        pass_on(name, target)

    for part in range(PARTS):
        piece = shard.at[pl.ds((x * 2 + c) * quarter + part * run, run)]
        far = shard.at[pl.ds(((1 - x) * 2 + c) * quarter + part * run, run)]
        for r in STEPS:
            send(("z", r, part), piece, place(z, y, x, part), dev(x, y, (z + r) % 4, c))
        send(("y", 0, part), piece, place(z, y, x, part), side_y)
        send(("d", 0, part), far, place(z, y, 1 - x, part), side_y)
    head_in.start()
    tail_in.start()

    rows_out = (((0,), (0,)), ((), ()))

    def gram_add(z_at, y_at, x_at, part):
        first = first_block(z_at, y_at, x_at, part, c)
        for k in range(run):
            rows = items[first + k]
            gram[...] += lax.dot_general(rows, rows, rows_out, preferred_element_type=jnp.float32)

    def gram_planes(places, part):
        def body(r, carry):
            for y_at, x_at in places:
                gram_add((z + 4 - r) % 4, y_at, x_at, part)
            return carry

        lax.fori_loop(1, 4, body, 0)

    def column_part(part):
        for r in STEPS:
            here = place((z + 4 - r) % 4, y, x, part)
            arrive(("z", r, part), here)
            send(("x", r, part), here, here, side_x)
            send(("y", r, part), here, here, side_y)
            pass_on(("z", r, part), here)
        take(("y", 0, part), place(z, 1 - y, x, part))
        take(("d", 0, part), place(z, 1 - y, 1 - x, part))

    def side_part(part):
        for r in STEPS:
            plane = (z + 4 - r) % 4
            from_x, from_y = place(plane, y, 1 - x, part), place(plane, 1 - y, x, part)
            by_x = r == 1 or (r == 2 and part % 2 == 0) or (r == 3 and part % 2 == 0)
            arrive(("x", r, part), from_x)
            if not by_x:
                send(("d", r, part), from_x, from_x, side_y)
            pass_on(("x", r, part), from_x)
            arrive(("y", r, part), from_y)
            if by_x:
                send(("d", r, part), from_y, from_y, side_x)
            pass_on(("y", r, part), from_y)

    def corner_part(part):
        for r in STEPS:
            take(("d", r, part), place((z + 4 - r) % 4, 1 - y, 1 - x, part))

    def weigh(held, base):
        def body(g, carry):
            weight_list, rated_list = [], []
            for k in range(GROUP):
                count = held[g * GROUP + k].astype(jnp.float32)
                weight = conf_alpha * count
                weight_list.append(weight.astype(jnp.bfloat16))
                rated_list.append(jnp.where(count > 0, 1.0 + weight, 0.0).astype(jnp.bfloat16))
            weights[base + g] = jnp.concatenate(weight_list, axis=1)
            rated[base + g] = jnp.concatenate(rated_list, axis=1)
            return carry

        lax.fori_loop(0, held.shape[0] // GROUP, body, 0)

    gram[...] = jnp.zeros_like(gram)
    own.wait()
    for part in range(PARTS + 2):
        if part < PARTS:
            column_part(part)
        if 1 <= part <= PARTS:
            side_part(part - 1)
        if part >= 2:
            corner_part(part - 2)
        if part < PARTS:
            gram_planes([(y, x)], part)
            for y_at, x_at in ((y, x), (y, 1 - x), (1 - y, x), (1 - y, 1 - x)):
                gram_add(z, y_at, x_at, part)
        if 1 <= part <= PARTS:
            gram_planes([(y, 1 - x), (1 - y, x)], part - 1)
        if part == 0:
            head_in.wait()
            weigh(head_held, 0)
        if part == 1:
            tail_in.wait()
            weigh(tail_held, heads // GROUP)
        if part >= 2:
            gram_planes([(1 - y, 1 - x)], part - 2)
    send(("gram",), gram, gram_other, side_c)
    arrive(("gram",), gram_other)

    last = (((1,), (1,)), ((), ()))

    def dense_part(vector):
        image = jnp.dot(
            vector,
            gram[...] + gram_other[...],
            precision=lax.Precision.HIGHEST,
            preferred_element_type=jnp.float32,
        )
        return image + ridge_term * vector

    start_vec = start[...]
    acc[...] = -dense_part(start_vec)
    rounded_start = start_vec.astype(jnp.bfloat16)
    for part in range(PARTS):
        arrive(("c", "y", 0, part), other_core(z, 1 - y, x, part))
        arrive(("c", "d", 0, part), other_core(z, 1 - y, 1 - x, part))
        for r in STEPS:
            plane = (z + 4 - r) % 4
            arrive(("c", "z", r, part), other_core(plane, y, x, part))
            arrive(("c", "x", r, part), other_core(plane, y, 1 - x, part))
            arrive(("c", "y", r, part), other_core(plane, 1 - y, x, part))
            arrive(("c", "d", r, part), other_core(plane, 1 - y, 1 - x, part))

    def each_group(step):
        for ids, count, base in ((head_ids, heads, 0), (tail_ids, tails, heads // GROUP)):

            def body(g, carry, ids=ids, base=base):
                rows = jnp.concatenate([items[ids[g * GROUP + k]] for k in range(GROUP)], axis=0)
                step(base + g, rows)
                return carry

            lax.fori_loop(0, count // GROUP, body, 0)

    def data_part(rounded, rows, g):
        scores = lax.dot_general(rounded, rows, last, preferred_element_type=jnp.float32)
        scaled = (scores * weights[g].astype(jnp.float32)).astype(jnp.bfloat16)
        return jnp.dot(scaled, rows, preferred_element_type=jnp.float32)

    def first_step(g, rows):
        target = jnp.dot(rated[g], rows, preferred_element_type=jnp.float32)
        acc[...] += target - data_part(rounded_start, rows, g)

    each_group(first_step)

    def apply(vector):
        acc[...] = dense_part(vector)
        rounded = vector.astype(jnp.bfloat16)

        def step(g, rows):
            acc[...] += data_part(rounded, rows, g)

        each_group(step)
        return acc[...]

    solution = start_vec
    residual = acc[...]
    direction = residual
    norm_now = jnp.sum(residual * residual, axis=1, keepdims=True)
    for turn_index in range(ITERS):
        image_vec = apply(direction)
        step_size = norm_now / (jnp.sum(direction * image_vec, axis=1, keepdims=True) + epsilon)
        solution = solution + step_size * direction
        residual = residual - step_size * image_vec
        if turn_index + 1 < ITERS:
            norm_next = jnp.sum(residual * residual, axis=1, keepdims=True)
            direction = residual + norm_next / (norm_now + epsilon) * direction
            norm_now = norm_next
    out[...] = solution
    residual_out[...] = residual
    for made in started:
        made.wait_send()


def local_gathered(user_factors, item_factors, head_ids, tail_ids, head_counts, tail_counts):
    size, width = head_counts.shape[-1], item_factors.shape[1]
    heads, tails = head_counts.shape[1], tail_counts.shape[1]
    shard_blocks = item_factors.shape[0] // size
    groups = (heads + tails) // GROUP
    smem = pl.BlockSpec(memory_space=pltpu.SMEM)
    vmem = pl.BlockSpec(memory_space=pltpu.VMEM)
    anywhere = pl.BlockSpec(memory_space=pl.ANY)
    shape = jax.ShapeDtypeStruct(user_factors.shape, jnp.float32)
    return pl.pallas_call(
        solve_kernel,
        out_shape=(shape, shape),
        in_specs=[smem, smem, vmem, anywhere, anywhere, anywhere],
        out_specs=(vmem, vmem),
        scratch_shapes=[
            pltpu.VMEM((lax.axis_size("item") * shard_blocks, size, width), jnp.bfloat16),
            pltpu.VMEM((heads, size, size), jnp.int32),
            pltpu.VMEM((tails, size, size), jnp.int32),
            pltpu.VMEM((groups, size, GROUP * size), jnp.bfloat16),
            pltpu.VMEM((groups, size, GROUP * size), jnp.bfloat16),
            pltpu.VMEM((width, width), jnp.float32),
            pltpu.VMEM((width, width), jnp.float32),
            pltpu.VMEM((size, width), jnp.float32),
            pltpu.SemaphoreType.DMA((COPIES,)),
            pltpu.SemaphoreType.DMA((COPIES,)),
            pltpu.SemaphoreType.DMA((3,)),
        ],
        compiler_params=pltpu.CompilerParams(
            collective_id=0, has_side_effects=True, vmem_limit_bytes=52 * 1024 * 1024
        ),
    )(
        head_ids,
        tail_ids.reshape(-1),
        user_factors,
        item_factors.reshape(shard_blocks, size, width),
        head_counts[0],
        tail_counts[0],
    )


def solution(mesh):
    small = mesh.shape["user"] == 4 and mesh.shape["item"] == 8
    return jax.shard_map(
        local_gathered if small else local,
        mesh=mesh,
        in_specs=(
            P(("user", "item"), None),
            P("item", None),
            P(),
            P(("user", "item"), None),
            P(("user", "item"), None, None, None),
            P(("user", "item"), None, None, None),
        ),
        out_specs=(P(("user", "item"), None), P(("user", "item"), None)),
        check_vma=False,
    )
```

```python
import jax
import jax.numpy as jnp
from jax import lax
from jax.experimental import pallas as pl
from jax.experimental.pallas import tpu as pltpu
from jax.sharding import PartitionSpec as P

ITERS = 2


conf_alpha = 4.0
ridge_term = 0.1
epsilon = 1e-06


def apply_operator(vector, gram_matrix, item_tiles, weights):
    rounded = vector.astype(jnp.bfloat16)
    scores = jnp.einsum("uf,kif->kui", rounded, item_tiles, preferred_element_type=jnp.float32)
    scaled = (scores * weights).astype(jnp.bfloat16)
    data_term = jnp.einsum("kui,kif->uf", scaled, item_tiles, preferred_element_type=jnp.float32)
    gram_term = jnp.dot(vector, gram_matrix, precision=lax.Precision.HIGHEST)
    return gram_term + ridge_term * vector + data_term


def solve_block(start_vec, gram_matrix, item_tiles, counts):
    count_float = counts.astype(jnp.float32)
    weights = (conf_alpha * count_float).astype(jnp.bfloat16)
    rated_weight = jnp.where(counts > 0, 1.0 + conf_alpha * count_float, 0.0).astype(jnp.bfloat16)
    rhs = jnp.einsum("kui,kif->uf", rated_weight, item_tiles, preferred_element_type=jnp.float32)
    solution = start_vec
    residual = rhs - apply_operator(solution, gram_matrix, item_tiles, weights)
    direction = residual
    norm_now = jnp.sum(residual * residual, axis=1, keepdims=True)
    for turn_index in range(ITERS):
        image_vec = apply_operator(direction, gram_matrix, item_tiles, weights)
        step_size = norm_now / (jnp.sum(direction * image_vec, axis=1, keepdims=True) + epsilon)
        solution = solution + step_size * direction
        residual = residual - step_size * image_vec
        if turn_index + 1 < ITERS:
            norm_next = jnp.sum(residual * residual, axis=1, keepdims=True)
            direction = residual + norm_next / (norm_now + epsilon) * direction
            norm_now = norm_next
    return (solution, residual)


def take_blocks(blocks, ids):
    return jnp.stack(
        [lax.dynamic_index_in_dim(blocks, ids[k], 0, keepdims=False) for k in range(ids.shape[0])]
    )


def local(user_factors, item_factors, head_ids, tail_ids, head_counts, tail_counts):
    item_count = lax.axis_size("item")
    user_count = lax.axis_size("user")
    block_size = head_counts.shape[-1]
    rank_width = item_factors.shape[1]
    shard_blocks = item_factors.shape[0] // block_size
    blocks = item_factors.reshape(shard_blocks, block_size, rank_width)
    my_item = lax.axis_index("item")
    contract = (((0,), (0,)), ((), ()))
    slice_rows = item_factors.shape[0] // user_count
    rows_part = lax.dynamic_slice_in_dim(
        item_factors, lax.axis_index("user") * slice_rows, slice_rows, 0
    )
    local_gram = lax.dot_general(rows_part, rows_part, contract, preferred_element_type=jnp.float32)
    gram_matrix = lax.psum(local_gram, ("user", "item"))
    head_owner = head_ids // shard_blocks
    head_local = head_ids % shard_blocks
    owned = head_owner == my_item
    picked = jnp.where(owned[:, None, None], take_blocks(blocks, head_local), jnp.zeros((), jnp.bfloat16))
    head_rows = lax.psum(picked, "item").astype(jnp.float32).astype(jnp.bfloat16)
    wanted = tail_ids.reshape(-1)
    length = wanted.shape[0]
    capacity = 2 * length // item_count
    owner_of = wanted // shard_blocks
    local_of = wanted % shard_blocks
    same_owner = owner_of[:, None] == owner_of[None, :]
    positions = jnp.arange(length, dtype=jnp.int32)
    earlier = positions[:, None] > positions[None, :]
    place_index = jnp.sum((same_owner & earlier).astype(jnp.int32), axis=1)
    slot_index = owner_of * capacity + place_index
    slot_table = slot_index[:, None] == jnp.arange(item_count * capacity, dtype=jnp.int32)[None, :]
    requests = jnp.sum(jnp.where(slot_table, local_of[:, None], 0), axis=0)
    requests = requests.reshape(item_count, capacity)
    asked = lax.all_to_all(requests, "item", split_axis=0, concat_axis=0, tiled=True)
    served = take_blocks(blocks, asked.reshape(-1)).reshape(item_count, capacity, block_size, rank_width)
    arrived_tail = lax.all_to_all(served, "item", split_axis=0, concat_axis=0, tiled=True)
    tail_rows = take_blocks(
        arrived_tail.reshape(item_count * capacity, block_size, rank_width), slot_index
    )
    local_blocks = tail_ids.shape[0]
    tail_tiles = tail_rows.reshape(local_blocks, tail_ids.shape[1], block_size, rank_width)
    start_blocks = user_factors.reshape(local_blocks, block_size, rank_width)

    def one_block(block_args):
        start_vec, tail_part_rows, head_part, tail_part = block_args
        item_tiles = jnp.concatenate([head_rows, tail_part_rows], axis=0)
        counts = jnp.concatenate([head_part, tail_part], axis=0)
        return solve_block(start_vec, gram_matrix, item_tiles, counts)

    solution, residual = lax.map(one_block, (start_blocks, tail_tiles, head_counts, tail_counts))
    return (
        solution.reshape(local_blocks * block_size, rank_width),
        residual.reshape(local_blocks * block_size, rank_width),
    )


PARTS = 4
STEPS = (1, 3, 2)
GROUP = 4
COPIES = PARTS * (3 + 3 + 4 + 4 + 14 + 2) + 1


def solve_kernel(
    head_ids, tail_ids, start, shard, head_counts, tail_counts, out, residual_out,
    items, head_held, tail_held, weights, rated, gram, gram_other, acc,
    send_sem, recv_sem, own_sem,
):
    user, item = lax.axis_index("user"), lax.axis_index("item")
    x, c = user // 2, user % 2
    z, y = item // 2, item % 2
    shard_blocks, size, width = shard.shape
    quarter = shard_blocks // 4
    run = quarter // PARTS
    heads, tails = head_counts.shape[0], tail_counts.shape[0]

    def dev(x_at, y_at, z_at, c_at):
        return (x_at * 2 + c_at, z_at * 2 + y_at)

    side_x, side_y, side_c = dev(1 - x, y, z, c), dev(x, 1 - y, z, c), dev(x, y, z, 1 - c)
    barrier = pltpu.get_barrier_semaphore()
    for other in [side_x, side_y, side_c] + [dev(x, y, (z + r) % 4, c) for r in STEPS]:
        pl.semaphore_signal(barrier, inc=1, device_id=other, device_id_type=pl.DeviceIdType.MESH)
    own = pltpu.make_async_copy(shard, items.at[pl.ds(item * shard_blocks, shard_blocks)], own_sem.at[0])
    head_in = pltpu.make_async_copy(head_counts, head_held, own_sem.at[1])
    tail_in = pltpu.make_async_copy(tail_counts, tail_held, own_sem.at[2])
    own.start()
    pl.semaphore_wait(barrier, 6)

    def first_block(z_at, y_at, x_at, part, core):
        return (z_at * 2 + y_at) * shard_blocks + (x_at * 2 + core) * quarter + part * run

    def place(z_at, y_at, x_at, part):
        return items.at[pl.ds(first_block(z_at, y_at, x_at, part, c), run)]

    def other_core(z_at, y_at, x_at, part):
        return items.at[pl.ds(first_block(z_at, y_at, x_at, part, 1 - c), run)]

    slots = {}

    def slot(name):
        return slots.setdefault(name, len(slots))

    def copy(name, source, target, device):
        return pltpu.make_async_remote_copy(
            src_ref=source,
            dst_ref=target,
            send_sem=send_sem.at[slot(name)],
            recv_sem=recv_sem.at[slot(name)],
            device_id=device,
            device_id_type=pl.DeviceIdType.MESH,
        )

    started, started_where = [], []

    def send(name, source, target, device):
        made = copy(name, source, target, device)
        made.start()
        started.append(made)

    def send_where(flag, name, source, target, device, via=None):
        if flag is True:
            return send(name, source, target, device)
        made = pltpu.make_async_remote_copy(
            src_ref=source,
            dst_ref=target,
            send_sem=send_sem.at[slot(via or name)],
            recv_sem=recv_sem.at[slot(name)],
            device_id=device,
            device_id_type=pl.DeviceIdType.MESH,
        )
        pl.when(flag)(made.start)
        started_where.append((flag, made))

    def not_near(r):
        return {1: z == 0, 2: True, 3: z == 3}[r]

    def arrive(name, target):
        copy(name, target, target, side_c).wait_recv()

    def pass_on(name, target):
        send(("c",) + name, target, target, side_c)

    def take(name, target):
        arrive(name, target)
        pass_on(name, target)

    for part in range(PARTS):
        piece = shard.at[pl.ds((x * 2 + c) * quarter + part * run, run)]
        far = shard.at[pl.ds(((1 - x) * 2 + c) * quarter + part * run, run)]
        for r in STEPS:
            send(("z", r, part), piece, place(z, y, x, part), dev(x, y, (z + r) % 4, c))
        send(("y", 0, part), piece, place(z, y, x, part), side_y)
        send(("d", 0, part), far, place(z, y, 1 - x, part), side_y)
    head_in.start()
    tail_in.start()

    rows_out = (((0,), (0,)), ((), ()))

    def gram_add(z_at, y_at, x_at, part):
        first = first_block(z_at, y_at, x_at, part, c)
        for k in range(run):
            rows = items[first + k]
            gram[...] += lax.dot_general(rows, rows, rows_out, preferred_element_type=jnp.float32)

    def gram_planes(places, part):
        def body(r, carry):
            for y_at, x_at in places:
                gram_add((z + 4 - r) % 4, y_at, x_at, part)
            return carry

        lax.fori_loop(1, 4, body, 0)

    def column_part(part):
        for r in STEPS:
            here = place((z + 4 - r) % 4, y, x, part)
            arrive(("z", r, part), here)
            send(("x", r, part), here, here, side_x)
            send(("y", r, part), here, here, side_y)
            pass_on(("z", r, part), here)
        take(("y", 0, part), place(z, 1 - y, x, part))
        corner = place(z, 1 - y, 1 - x, part)
        arrive(("d", 0, part), corner)
        send_where(z <= 2, ("d", 1, part), corner, corner, dev(x, y, (z + 1) % 4, c), ("u", part))
        send_where(z >= 1, ("d", 3, part), corner, corner, dev(x, y, (z + 3) % 4, c), ("v", part))
        pass_on(("d", 0, part), corner)

    def side_part(part):
        for r in STEPS:
            plane = (z + 4 - r) % 4
            from_x, from_y = place(plane, y, 1 - x, part), place(plane, 1 - y, x, part)
            arrive(("x", r, part), from_x)
            pass_on(("x", r, part), from_x)
            arrive(("y", r, part), from_y)
            send_where(not_near(r), ("d", r, part), from_y, from_y, side_x)
            pass_on(("y", r, part), from_y)

    def corner_part(part):
        for r in STEPS:
            take(("d", r, part), place((z + 4 - r) % 4, 1 - y, 1 - x, part))

    def weigh(held, base):
        def body(g, carry):
            weight_list, rated_list = [], []
            for k in range(GROUP):
                count = held[g * GROUP + k].astype(jnp.float32)
                weight = conf_alpha * count
                weight_list.append(weight.astype(jnp.bfloat16))
                rated_list.append(jnp.where(count > 0, 1.0 + weight, 0.0).astype(jnp.bfloat16))
            weights[base + g] = jnp.concatenate(weight_list, axis=1)
            rated[base + g] = jnp.concatenate(rated_list, axis=1)
            return carry

        lax.fori_loop(0, held.shape[0] // GROUP, body, 0)

    gram[...] = jnp.zeros_like(gram)
    own.wait()
    for part in range(PARTS + 2):
        if part < PARTS:
            column_part(part)
        if 1 <= part <= PARTS:
            side_part(part - 1)
        if part >= 2:
            corner_part(part - 2)
        if part < PARTS:
            gram_planes([(y, x)], part)
            for y_at, x_at in ((y, x), (y, 1 - x), (1 - y, x), (1 - y, 1 - x)):
                gram_add(z, y_at, x_at, part)
        if 1 <= part <= PARTS:
            gram_planes([(y, 1 - x), (1 - y, x)], part - 1)
        if part == 0:
            head_in.wait()
            weigh(head_held, 0)
        if part == 1:
            tail_in.wait()
            weigh(tail_held, heads // GROUP)
        if part >= 2:
            gram_planes([(1 - y, 1 - x)], part - 2)
    send(("gram",), gram, gram_other, side_c)
    arrive(("gram",), gram_other)

    last = (((1,), (1,)), ((), ()))

    def dense_part(vector):
        image = jnp.dot(
            vector,
            gram[...] + gram_other[...],
            precision=lax.Precision.HIGHEST,
            preferred_element_type=jnp.float32,
        )
        return image + ridge_term * vector

    start_vec = start[...]
    acc[...] = -dense_part(start_vec)
    rounded_start = start_vec.astype(jnp.bfloat16)
    for part in range(PARTS):
        arrive(("c", "y", 0, part), other_core(z, 1 - y, x, part))
        arrive(("c", "d", 0, part), other_core(z, 1 - y, 1 - x, part))
        for r in STEPS:
            plane = (z + 4 - r) % 4
            arrive(("c", "z", r, part), other_core(plane, y, x, part))
            arrive(("c", "x", r, part), other_core(plane, y, 1 - x, part))
            arrive(("c", "y", r, part), other_core(plane, 1 - y, x, part))
            arrive(("c", "d", r, part), other_core(plane, 1 - y, 1 - x, part))

    def each_group(step):
        for ids, count, base in ((head_ids, heads, 0), (tail_ids, tails, heads // GROUP)):

            def body(g, carry, ids=ids, base=base):
                rows = jnp.concatenate([items[ids[g * GROUP + k]] for k in range(GROUP)], axis=0)
                step(base + g, rows)
                return carry

            lax.fori_loop(0, count // GROUP, body, 0)

    def data_part(rounded, rows, g):
        scores = lax.dot_general(rounded, rows, last, preferred_element_type=jnp.float32)
        scaled = (scores * weights[g].astype(jnp.float32)).astype(jnp.bfloat16)
        return jnp.dot(scaled, rows, preferred_element_type=jnp.float32)

    def first_step(g, rows):
        target = jnp.dot(rated[g], rows, preferred_element_type=jnp.float32)
        acc[...] += target - data_part(rounded_start, rows, g)

    each_group(first_step)

    def apply(vector):
        acc[...] = dense_part(vector)
        rounded = vector.astype(jnp.bfloat16)

        def step(g, rows):
            acc[...] += data_part(rounded, rows, g)

        each_group(step)
        return acc[...]

    solution = start_vec
    residual = acc[...]
    direction = residual
    norm_now = jnp.sum(residual * residual, axis=1, keepdims=True)
    for turn_index in range(ITERS):
        image_vec = apply(direction)
        step_size = norm_now / (jnp.sum(direction * image_vec, axis=1, keepdims=True) + epsilon)
        solution = solution + step_size * direction
        residual = residual - step_size * image_vec
        if turn_index + 1 < ITERS:
            norm_next = jnp.sum(residual * residual, axis=1, keepdims=True)
            direction = residual + norm_next / (norm_now + epsilon) * direction
            norm_now = norm_next
    out[...] = solution
    residual_out[...] = residual
    for made in started:
        made.wait_send()
    for flag, made in started_where:
        pl.when(flag)(made.wait_send)


def local_gathered(user_factors, item_factors, head_ids, tail_ids, head_counts, tail_counts):
    size, width = head_counts.shape[-1], item_factors.shape[1]
    heads, tails = head_counts.shape[1], tail_counts.shape[1]
    shard_blocks = item_factors.shape[0] // size
    groups = (heads + tails) // GROUP
    smem = pl.BlockSpec(memory_space=pltpu.SMEM)
    vmem = pl.BlockSpec(memory_space=pltpu.VMEM)
    anywhere = pl.BlockSpec(memory_space=pl.ANY)
    shape = jax.ShapeDtypeStruct(user_factors.shape, jnp.float32)
    return pl.pallas_call(
        solve_kernel,
        out_shape=(shape, shape),
        in_specs=[smem, smem, vmem, anywhere, anywhere, anywhere],
        out_specs=(vmem, vmem),
        scratch_shapes=[
            pltpu.VMEM((lax.axis_size("item") * shard_blocks, size, width), jnp.bfloat16),
            pltpu.VMEM((heads, size, size), jnp.int32),
            pltpu.VMEM((tails, size, size), jnp.int32),
            pltpu.VMEM((groups, size, GROUP * size), jnp.bfloat16),
            pltpu.VMEM((groups, size, GROUP * size), jnp.bfloat16),
            pltpu.VMEM((width, width), jnp.float32),
            pltpu.VMEM((width, width), jnp.float32),
            pltpu.VMEM((size, width), jnp.float32),
            pltpu.SemaphoreType.DMA((COPIES,)),
            pltpu.SemaphoreType.DMA((COPIES,)),
            pltpu.SemaphoreType.DMA((3,)),
        ],
        compiler_params=pltpu.CompilerParams(
            collective_id=0, has_side_effects=True, vmem_limit_bytes=52 * 1024 * 1024
        ),
    )(
        head_ids,
        tail_ids.reshape(-1),
        user_factors,
        item_factors.reshape(shard_blocks, size, width),
        head_counts[0],
        tail_counts[0],
    )


def solution(mesh):
    small = mesh.shape["user"] == 4 and mesh.shape["item"] == 8
    return jax.shard_map(
        local_gathered if small else local,
        mesh=mesh,
        in_specs=(
            P(("user", "item"), None),
            P("item", None),
            P(),
            P(("user", "item"), None),
            P(("user", "item"), None, None, None),
            P(("user", "item"), None, None, None),
        ),
        out_specs=(P(("user", "item"), None), P(("user", "item"), None)),
        check_vma=False,
    )
```
